512 devices in a mesh: mem: 16 (over x, y_lo, core), ocn: 32 (over y_hi, z).
Axes of the slice: x: 4, y: 8 (y_hi: 4, y_lo: 2; y = y_hi * 2 + y_lo), z: 8, core: 2. Of those that a mesh axis runs over, the one named last changes fastest.
Arguments:
- panel: bfloat16 [65536, 1024], P('mem', 'ocn'), may hold values from -40 to 40
- ocean: bfloat16 [65536, 8192], P('mem', 'ocn'), may hold values from -100 to 100
- cutoff: int32 [16, 64], P('mem', 'ocn'), may hold values 0 or 1
- factor_index: int32 [16, 64], P('mem', 'ocn'), may hold values from 0 to 7
- factor_table: float32 [8], replicated, may hold values from 0.5 to 2
Outputs:
- inflated: float32 [1024, 8192], P('mem', 'ocn')
The draws below stay inside these ranges and needn't reach their ends.
All inputs are finite; a program needn't handle non-finite values. No bound on the sum of `cutoff` on one device may be relied on, other than what follows from the above.
Results may differ from the reference program's by a relative error of at most 0.0003.
Values may be sent and summed in bfloat16 or wider, within the bound.
No kernel may reach another device: no remote copies, remote signals or barrier semaphores. Data moves between devices by JAX's collectives and lax.ppermute only.
A program may use at most 64 MiB of HBM per device.

```python
import math
import jax
import jax.numpy as jnp
from jax import lax

VD = 256
R = 1024
TR = 64
TV = 128
NF = 8
MEMBERS = 65536
OCEAN_VARIABLES = 8192


def shared_field(key):
    return jax.random.truncated_normal(key, -4.0, 4.0, (MEMBERS, R), jnp.float32)


def draw_panel(key, part):
    field = shared_field(key)
    key = jax.random.fold_in(key, 11)
    scale_factor = jnp.exp(jax.random.uniform(key, (R,), jnp.float32, 0.0, math.log(10.0)))
    return (field * scale_factor).astype(jnp.bfloat16)


def draw_ocean(key, part):
    field = shared_field(key)
    key = jax.random.fold_in(key, 23)
    noise_key, coefficient_key, scale_key = jax.random.split(key, 3)
    coef = jax.random.uniform(coefficient_key, (OCEAN_VARIABLES,), jnp.float32, -1.5, 1.5)
    noise = jax.random.truncated_normal(noise_key, -4.0, 4.0, (MEMBERS, OCEAN_VARIABLES), jnp.float32)
    scale_factor = jnp.exp(jax.random.uniform(scale_key, (OCEAN_VARIABLES,), jnp.float32, 0.0, math.log(10.0)))
    tiled = jnp.tile(field, (1, OCEAN_VARIABLES // R))
    return ((noise + coef * tiled) * scale_factor).astype(jnp.bfloat16)


def place_ends(array, own_key, least, largest):
    index_at = [jax.random.randint(jax.random.fold_in(own_key, axis), (), 0, length) for axis, length in enumerate(array.shape)]
    widest = array.shape.index(max(array.shape))
    beside = index_at[:widest] + [(index_at[widest] + 1) % array.shape[widest]] + index_at[widest + 1:]
    return array.at[tuple(index_at)].set(least).at[tuple(beside)].set(largest)


def setup_inputs(seed: int = 0) -> dict:
    key_of = jax.random.split(jax.random.key(seed), 6)
    panel = draw_panel(jax.random.fold_in(key_of[5], 71), 0)
    ocean = draw_ocean(jax.random.fold_in(key_of[5], 71), 0)
    cutoff = place_ends((jax.random.randint(key_of[2], (R // TR, OCEAN_VARIABLES // TV), 0, 4) < 3).astype(jnp.int32), jax.random.fold_in(key_of[2], 1), 0, 1)
    factor_index = place_ends(jax.random.randint(key_of[3], (R // TR, OCEAN_VARIABLES // TV), 0, NF), jax.random.fold_in(key_of[3], 1), 0, NF - 1).astype(jnp.int32)
    factor_table = jnp.clip(jnp.exp(jax.random.uniform(key_of[4], (NF,), jnp.float32, math.log(0.5), math.log(2.0))), 0.5, 2.0)
    return dict(panel=panel, ocean=ocean, cutoff=cutoff, factor_index=factor_index, factor_table=factor_table)


def reference(panel, ocean, cutoff, factor_index, factor_table):
    members = panel.shape[0]
    panel_f = panel.astype(jnp.float32)
    rowsq = lax.optimization_barrier(jnp.sum(panel_f * panel_f, axis=0))
    nblocks = ocean.shape[1] // VD

    def one_block(index):
        block = lax.dynamic_slice_in_dim(ocean, (index * VD).astype(jnp.int32), VD, 1).astype(jnp.float32)
        prod = jnp.dot(panel_f.T, block, precision=lax.Precision.HIGHEST)
        return (prod, lax.optimization_barrier(jnp.sum(block * block, axis=0)))
    prods, sqs = lax.map(one_block, jnp.arange(nblocks, dtype=jnp.int32))
    covsum = jnp.moveaxis(prods, 0, 1).reshape(panel.shape[1], nblocks * VD)
    colsq = sqs.reshape(nblocks * VD)
    vx = rowsq / (members - 1.0) + 1e-06
    vy = colsq / (members - 1.0) + 1e-06
    corr = covsum / (members - 1.0) / jnp.sqrt(vx[:, None] * vy[None, :])
    picks = factor_index[..., None] == jnp.arange(NF, dtype=jnp.int32)
    weight = cutoff.astype(jnp.float32) * lax.optimization_barrier(jnp.sum(jnp.where(picks, factor_table, jnp.float32(0.0)), axis=-1))
    rb, vb = weight.shape
    out = corr.reshape(rb, TR, vb, TV) * weight[:, None, :, None]
    return out.reshape(rb * TR, vb * TV)
```

```python
import jax
import jax.numpy as jnp
from jax import lax
from jax.experimental import pallas as pl
from jax.experimental.pallas import tpu as pltpu
from jax.sharding import PartitionSpec as P

TR = 64
TV = 128
NZ = 8
NY = 4
EXTRA = 8


def z_shift(x, d):
    perm = [(o, (o // NZ) * NZ + (o % NZ + d) % NZ) for o in range(NY * NZ)]
    return lax.ppermute(x, "ocn", perm)


def y_shift(x, d):
    perm = [(o, ((o // NZ + d) % NY) * NZ + o % NZ) for o in range(NY * NZ)]
    return lax.ppermute(x, "ocn", perm)


def z_ring(x, n_up, n_down):
    got = []
    up = down = x
    for s in range(1, max(n_up, n_down) + 1):
        if s <= n_up:
            up = z_shift(up, 1)
            got.append((up, -s))
        if s <= n_down:
            down = z_shift(down, -1)
            got.append((down, s))
    return got


def cross_kernel(places, *refs):
    n = len(places)
    blocks, ocean_ref, out_ref, rows_ref, sem = refs[:n], refs[n], refs[n + 1], refs[n + 2], refs[n + 3]
    o = lax.axis_index("ocn")
    y, z = o // NZ, lax.rem(o, NZ)
    copies = []
    for ref, (groups, dz) in zip(blocks, places):
        per = ref.shape[0] // len(groups)
        for g, dy in enumerate(groups):
            origin = lax.rem(y + (dy + NY), NY) * NZ + lax.rem(z + (dz + NZ), NZ)
            start = pl.multiple_of(origin * per, per)
            copies.append(
                pltpu.make_async_copy(
                    ref.at[pl.ds(g * per, per)], rows_ref.at[pl.ds(start, per)], sem.at[len(copies)]
                )
            )
    for c in copies:
        c.start()
    ocean = ocean_ref[...]
    ocean_f = ocean.astype(jnp.float32)
    colsq = jnp.sum(ocean_f * ocean_f, axis=0, keepdims=True)
    for c in copies:
        c.wait()
    n_own = out_ref.shape[0]
    own = rows_ref.shape[0] // n_own
    per_tile = 4
    line = lax.broadcasted_iota(jnp.int32, (EXTRA, ocean.shape[1]), 0)
    eye = lax.broadcasted_iota(jnp.int32, (own, 128), 0) == lax.broadcasted_iota(jnp.int32, (own, 128), 1)

    @pl.loop(0, n_own // per_tile)
    def _(t):
        first = pl.multiple_of(t * (per_tile * own), per_tile * own)
        tile = rows_ref[pl.ds(first, per_tile * own), :]
        cov = jnp.dot(tile, ocean_ref[...], preferred_element_type=jnp.float32)
        tile_f = tile.astype(jnp.float32)
        rowsq = jnp.sum(tile_f * tile_f, axis=1, keepdims=True)
        for k in range(per_tile):
            part = slice(k * own, (k + 1) * own)
            across = jnp.sum(jnp.where(eye, rowsq[part], 0.0), axis=0, keepdims=True)
            across = jnp.concatenate([across, jnp.zeros_like(across)], axis=1)
            out_ref[t * per_tile + k, :own, :] = cov[part]
            out_ref[t * per_tile + k, own:, :] = jnp.where(line == 0, across, jnp.where(line == 1, colsq, 0.0))


def cross(pieces, ocean, rows_all, n_mem):
    places = [(groups, dz) for _, groups, dz in pieces]
    n_copies = sum(len(groups) for groups, _ in places)
    members, cols = ocean.shape
    own = rows_all // n_mem
    return pl.pallas_call(
        lambda *refs: cross_kernel(places, *refs),
        out_shape=jax.ShapeDtypeStruct((n_mem, own + EXTRA, cols), jnp.float32),
        in_specs=[pl.BlockSpec(memory_space=pl.ANY)] * len(pieces) + [pl.BlockSpec(memory_space=pltpu.VMEM)],
        out_specs=pl.BlockSpec(memory_space=pltpu.VMEM),
        scratch_shapes=[pltpu.VMEM((rows_all, members), jnp.bfloat16), pltpu.SemaphoreType.DMA((n_copies,))],
        compiler_params=pltpu.CompilerParams(vmem_limit_bytes=32 * 1024 * 1024),
        cost_estimate=pl.CostEstimate(
            flops=2 * rows_all * members * cols, bytes_accessed=2 * members * (rows_all + cols), transcendentals=0
        ),
    )(*[a for a, _, _ in pieces], ocean)


def finish_kernel(members, parts_ref, cutoff_ref, index_ref, table_ref, out_ref):
    own, cols = out_ref.shape
    total = jnp.sum(parts_ref[...], axis=0)
    eye = lax.broadcasted_iota(jnp.int32, (own, 128), 0) == lax.broadcasted_iota(jnp.int32, (own, 128), 1)
    rowsq = jnp.sum(jnp.where(eye, total[own : own + 1, :128], 0.0), axis=1, keepdims=True)
    vx = rowsq / (members - 1.0) + 1e-06
    vy = total[own + 1 : own + 2] / (members - 1.0) + 1e-06
    corr = total[:own] / (members - 1.0) / jnp.sqrt(vx * vy)
    for i in range(own // TR):
        for j in range(cols // TV):
            weight = cutoff_ref[i, j].astype(jnp.float32) * table_ref[index_ref[i, j]]
            tile = (slice(i * TR, (i + 1) * TR), slice(j * TV, (j + 1) * TV))
            out_ref[tile] = corr[tile] * weight


def per_device(panel, ocean, cutoff, factor_index, factor_table):
    n_mem = lax.axis_size("mem")
    rows_all = panel.shape[1] * lax.axis_size("ocn")
    own_rows = rows_all // n_mem
    members = panel.shape[0] * n_mem
    mine = panel.T
    from_below = y_shift(mine, 1)
    from_above = y_shift(mine, -1)
    from_across = y_shift(mine, 2)
    first = jnp.concatenate([mine, from_below], axis=0)
    second = jnp.concatenate([from_above, from_across], axis=0)
    pieces = [(first, (0, -1), 0), (second, (1, 2), 0)]
    pieces += [(a, (0, -1), dz) for a, dz in z_ring(first, 4, 3)]
    pieces += [(a, (1, 2), dz) for a, dz in z_ring(second, 3, 4)]
    parts = cross(pieces, ocean, rows_all, n_mem)
    parts = lax.all_to_all(parts, "mem", split_axis=0, concat_axis=0, tiled=True)
    return pl.pallas_call(
        lambda *refs: finish_kernel(members, *refs),
        out_shape=jax.ShapeDtypeStruct((own_rows, ocean.shape[1]), jnp.float32),
        in_specs=[pl.BlockSpec(memory_space=pltpu.VMEM)] + [pl.BlockSpec(memory_space=pltpu.SMEM)] * 3,
        out_specs=pl.BlockSpec(memory_space=pltpu.VMEM),
        compiler_params=pltpu.CompilerParams(vmem_limit_bytes=16 * 1024 * 1024),
    )(parts, cutoff, factor_index, factor_table)


def solution(mesh):
    in_specs = (P("mem", "ocn"), P("mem", "ocn"), P("mem", "ocn"), P("mem", "ocn"), P())
    out_specs = P("mem", "ocn")
    return jax.shard_map(
        per_device, mesh=mesh, in_specs=in_specs, out_specs=out_specs, check_vma=False
    )
```

```python
import jax
import jax.numpy as jnp
from jax import lax
from jax.experimental import pallas as pl
from jax.experimental.pallas import tpu as pltpu
from jax.sharding import PartitionSpec as P

TR = 64
TV = 128
NZ = 8
NY = 4
EXTRA = 8


def z_shift(x, d):
    perm = [(o, (o // NZ) * NZ + (o % NZ + d) % NZ) for o in range(NY * NZ)]
    return lax.ppermute(x, "ocn", perm)


def y_shift(x, d):
    perm = [(o, ((o // NZ + d) % NY) * NZ + o % NZ) for o in range(NY * NZ)]
    return lax.ppermute(x, "ocn", perm)


def cross_kernel(groups, early, *refs):
    n = len(groups)
    blocks, ocean_ref = refs[:n], refs[n]
    out_ref, rows_ref, cov_ref, sq_ref, sem = refs[-5:]
    copies, placed, at = [], [], 0
    for ref, parts in zip(blocks, groups):
        copies.append(pltpu.make_async_copy(ref, rows_ref.at[pl.ds(at, ref.shape[0])], sem.at[len(copies)]))
        for dy, dz, first, count in parts:
            placed.append((at, dy, dz, first, count))
            at += count
    for c in copies:
        c.start()
    n_own, own = out_ref.shape[0], out_ref.shape[1] - EXTRA
    per = n_own * own // (NY * NZ)
    if early:
        ocean_f = ocean_ref[...].astype(jnp.float32)
        colsq = jnp.sum(ocean_f * ocean_f, axis=0, keepdims=True)
        line = lax.broadcasted_iota(jnp.int32, (EXTRA, colsq.shape[1]), 0)
        for m in range(n_own):
            out_ref[m, :own, :] = jnp.zeros((own, colsq.shape[1]), jnp.float32)
            out_ref[m, own:, :] = jnp.where(line == 2, colsq, 0.0)
    for c in copies:
        c.wait()
    tile = at // 2

    @pl.loop(0, 2)
    def _(t):
        part = pl.ds(pl.multiple_of(t * tile, 16), tile)
        rows = rows_ref[part, :]
        cov_ref[part, :] = jnp.dot(rows, ocean_ref[...], preferred_element_type=jnp.float32)
        rows_f = rows.astype(jnp.float32)
        sq_ref[part, :] = jnp.broadcast_to(jnp.sum(rows_f * rows_f, axis=1, keepdims=True), (tile, 128))

    o = lax.axis_index("ocn")
    y, z = o // NZ, lax.rem(o, NZ)
    for at, dy, dz, first, count in placed:
        origin = lax.rem(y + (dy + NY), NY) * NZ + lax.rem(z + (dz + NZ), NZ)
        owner, side = origin // 2, lax.rem(origin, 2)
        to = pl.ds(pl.multiple_of(side * per + first, 16), count)
        out_ref[owner, to, :] = cov_ref[at : at + count, :]
        row = lax.broadcasted_iota(jnp.int32, (count, 128), 0) + first
        lane = lax.broadcasted_iota(jnp.int32, (count, 128), 1)
        across = jnp.sum(jnp.where(row == lane, sq_ref[at : at + count, :], 0.0), axis=0, keepdims=True)
        line = lax.broadcasted_iota(jnp.int32, (EXTRA, 128), 0)
        out_ref[owner, own:, :128] += jnp.where(line == side, across, 0.0)


def cross(pieces, ocean, rows_all, n_mem, before=None):
    members, cols = ocean.shape
    rows = sum(a.shape[0] for a, _ in pieces)
    vmem = pl.BlockSpec(memory_space=pltpu.VMEM)
    args = [a for a, _ in pieces] + [ocean]
    specs = [pl.BlockSpec(memory_space=pl.ANY)] * len(pieces) + [vmem]
    if before is not None:
        args.append(before)
        specs.append(vmem)
    return pl.pallas_call(
        lambda *refs: cross_kernel([parts for _, parts in pieces], before is None, *refs),
        out_shape=jax.ShapeDtypeStruct((n_mem, rows_all // n_mem + EXTRA, cols), jnp.float32),
        in_specs=specs,
        out_specs=vmem,
        scratch_shapes=[
            pltpu.VMEM((rows, members), jnp.bfloat16),
            pltpu.VMEM((rows, cols), jnp.float32),
            pltpu.VMEM((rows, 128), jnp.float32),
            pltpu.SemaphoreType.DMA((len(pieces),)),
        ],
        input_output_aliases={} if before is None else {len(args) - 1: 0},
        compiler_params=pltpu.CompilerParams(vmem_limit_bytes=24 * 1024 * 1024),
        cost_estimate=pl.CostEstimate(
            flops=2 * rows * members * cols, bytes_accessed=2 * members * (rows + cols), transcendentals=0
        ),
    )(*args)


def finish_kernel(members, parts_ref, cutoff_ref, index_ref, table_ref, out_ref):
    own, cols = out_ref.shape
    total = jnp.sum(parts_ref[...], axis=0)
    eye = lax.broadcasted_iota(jnp.int32, (own, own), 0) == lax.broadcasted_iota(jnp.int32, (own, own), 1)
    half = own // 2
    across = jnp.concatenate([total[own : own + 1, :half], total[own + 1 : own + 2, :half]], axis=1)
    rowsq = jnp.sum(jnp.where(eye, across, 0.0), axis=1, keepdims=True)
    vx = rowsq / (members - 1.0) + 1e-06
    vy = total[own + 2 : own + 3] / (members - 1.0) + 1e-06
    corr = total[:own] / (members - 1.0) / jnp.sqrt(vx * vy)
    for i in range(own // TR):
        for j in range(cols // TV):
            weight = cutoff_ref[i, j].astype(jnp.float32) * table_ref[index_ref[i, j]]
            tile = (slice(i * TR, (i + 1) * TR), slice(j * TV, (j + 1) * TV))
            out_ref[tile] = corr[tile] * weight


def per_device(panel, ocean, cutoff, factor_index, factor_table):
    n_mem = lax.axis_size("mem")
    rows_all = panel.shape[1] * lax.axis_size("ocn")
    own_rows = rows_all // n_mem
    members = panel.shape[0] * n_mem
    mine = panel.T
    per = mine.shape[0]
    half = per // 2
    lo, hi = (0, half), (half, half)
    from_below = y_shift(mine, 1)
    from_above = y_shift(mine, -1)
    from_across = y_shift(mine, 2)
    own_up = z_shift(mine, 1)
    own_down = z_shift(mine, -1)

    first = [from_below, from_across[:half]]
    second = [from_above, from_across[half:]]
    up_1 = jnp.concatenate(first + [own_up[:half]], axis=0)
    up_2 = jnp.concatenate(second + [own_up[half:]], axis=0)
    down_1 = jnp.concatenate(first + [own_down[:half]], axis=0)
    down_2 = jnp.concatenate(second + [own_down[half:]], axis=0)
    both = per + half

    def parts_1(dz, own_dz=None):
        parts = [(-1, dz, 0, per), (2, dz, *lo)]
        return parts if own_dz is None else parts + [(0, own_dz, *lo)]

    def parts_2(dz, own_dz=None):
        parts = [(1, dz, 0, per), (2, dz, *hi)]
        return parts if own_dz is None else parts + [(0, own_dz, *hi)]

    early = [(mine, [(0, 0, 0, per)]), (up_1, parts_1(0, -1)), (up_2, parts_2(0, -1)), (own_down, [(0, 1, 0, per)])]
    for s in (1, 2):
        up_1, down_1 = z_shift(up_1, 1), z_shift(down_1, -1)
        up_2, down_2 = z_shift(up_2, 1), z_shift(down_2, -1)
        early += [(up_1, parts_1(-s, -s - 1)), (down_1, parts_1(s, s + 1))]
        early += [(up_2, parts_2(-s, -s - 1)), (down_2, parts_2(s, s + 1))]
    up_1, down_1 = z_shift(up_1, 1), z_shift(down_1[:both], -1)
    up_2, down_2 = z_shift(up_2[:both], 1), z_shift(down_2, -1)
    late = [(up_1, parts_1(-3, -4)), (down_1, parts_1(3)), (up_2, parts_2(-3)), (down_2, parts_2(3, 4))]
    late += [(z_shift(down_1, -1), parts_1(4)), (z_shift(up_2, 1), parts_2(4))]

    parts = cross(early, ocean, rows_all, n_mem)
    parts = cross(late, ocean, rows_all, n_mem, parts)
    parts = lax.all_to_all(parts, "mem", split_axis=0, concat_axis=0, tiled=True)
    return pl.pallas_call(
        lambda *refs: finish_kernel(members, *refs),
        out_shape=jax.ShapeDtypeStruct((own_rows, ocean.shape[1]), jnp.float32),
        in_specs=[pl.BlockSpec(memory_space=pltpu.VMEM)] + [pl.BlockSpec(memory_space=pltpu.SMEM)] * 3,
        out_specs=pl.BlockSpec(memory_space=pltpu.VMEM),
        compiler_params=pltpu.CompilerParams(vmem_limit_bytes=16 * 1024 * 1024),
    )(parts, cutoff, factor_index, factor_table)


def solution(mesh):
    in_specs = (P("mem", "ocn"), P("mem", "ocn"), P("mem", "ocn"), P("mem", "ocn"), P())
    out_specs = P("mem", "ocn")
    return jax.shard_map(
        per_device, mesh=mesh, in_specs=in_specs, out_specs=out_specs, check_vma=False
    )
```

```python
import functools

import jax
import jax.numpy as jnp
from jax import lax
from jax.experimental import pallas as pl
from jax.experimental.pallas import tpu as pltpu
from jax.sharding import PartitionSpec as P

TR = 64
TV = 128
NZ = 8
NY = 4
EXTRA = 8
TAIL = 768


def z_shift(x, d):
    perm = [(o, (o // NZ) * NZ + (o % NZ + d) % NZ) for o in range(NY * NZ)]
    return lax.ppermute(x, "ocn", perm)


def y_shift(x, d):
    perm = [(o, ((o // NZ + d) % NY) * NZ + o % NZ) for o in range(NY * NZ)]
    return lax.ppermute(x, "ocn", perm)


def z_spread(x):
    groups = [[y * NZ + z for z in range(NZ)] for y in range(NY)]
    copies = jnp.broadcast_to(x[None], (NZ,) + x.shape).reshape(NZ * x.shape[0], x.shape[1])
    return lax.all_to_all(copies, "ocn", split_axis=0, concat_axis=0, axis_index_groups=groups, tiled=True)


def own_sums(rows):
    rows_f = rows.astype(jnp.float32)
    return jnp.sum(rows_f * rows_f, axis=1, keepdims=True)


def along_lanes(column, first):
    shape = (column.shape[0], 128)
    here = lax.broadcasted_iota(jnp.int32, shape, 0) + first == lax.broadcasted_iota(jnp.int32, shape, 1)
    return jnp.sum(jnp.where(here, column, 0.0), axis=0, keepdims=True)


def tail_kernel(*refs):
    blocks, ocean_ref = refs[:NY], refs[NY]
    out_ref, rows_ref, sem = refs[-3:]
    y = lax.axis_index("ocn") // NZ
    rows_y = blocks[0].shape[0]
    copies = []
    for ref, dy in zip(blocks, (0, -1, 1, 2)):
        start = pl.multiple_of(lax.rem(y + (dy + NY), NY) * rows_y, rows_y)
        copies.append(pltpu.make_async_copy(ref, rows_ref.at[pl.ds(start, rows_y)], sem.at[len(copies)]))
    for c in copies:
        c.start()
    members, cols = ocean_ref.shape
    tail = rows_ref.shape[1]
    ocean_f = ocean_ref[...].astype(jnp.float32)
    colsq = jnp.sum(ocean_f * ocean_f, axis=0, keepdims=True)
    line = lax.broadcasted_iota(jnp.int32, (EXTRA, cols), 0)
    own = out_ref.shape[1] - EXTRA
    per_y = rows_y // own
    for c in copies:
        c.wait()

    @pl.loop(0, NY)
    def _(t):
        rows = rows_ref[pl.ds(pl.multiple_of(t * rows_y, rows_y), rows_y), :]
        cov = jnp.dot(rows, ocean_ref[members - tail :, :], preferred_element_type=jnp.float32)
        sq = own_sums(rows)
        for k in range(per_y):
            owner = t * per_y + k
            out_ref[owner, :own, :] = cov[k * own : (k + 1) * own]
            lines = jnp.where(line == 2, colsq, 0.0)
            for side in range(2):
                at = k * own + side * (own // 2)
                across = along_lanes(sq[at : at + own // 2], 0)
                across = jnp.concatenate([across, jnp.zeros((1, cols - 128), jnp.float32)], axis=1)
                lines = jnp.where(line == side, across, lines)
            out_ref[owner, own:, :] = lines


def head_kernel(groups, *refs):
    n = len(groups)
    blocks, ocean_ref = refs[:n], refs[n]
    out_ref, rows_ref, cov_ref, sq_ref, sem = refs[-5:]
    own = out_ref.shape[1] - EXTRA
    per = own // 2
    copies, placed = [], []
    for ref, parts in zip(blocks, groups):
        to = pl.ds(len(placed) * per, ref.shape[0])
        copies.append(pltpu.make_async_copy(ref, rows_ref.at[to], sem.at[len(copies)]))
        placed.extend(parts)
    for c in copies:
        c.start()
    for c in copies:
        c.wait()
    n_rows, head = rows_ref.shape
    tile = n_rows // 2

    @pl.loop(0, 2)
    def _(t):
        part = pl.ds(pl.multiple_of(t * tile, 16), tile)
        rows = rows_ref[part, :]
        cov_ref[part, :] = jnp.dot(rows, ocean_ref[:head, :], preferred_element_type=jnp.float32)
        sq_ref[part, :] = jnp.broadcast_to(own_sums(rows), (tile, 128))

    o = lax.axis_index("ocn")
    y, z = o // NZ, lax.rem(o, NZ)
    line = lax.broadcasted_iota(jnp.int32, (EXTRA, 128), 0)
    for i, (dy, dz) in enumerate(placed):
        origin = lax.rem(y + (dy + NY), NY) * NZ + lax.rem(z + (dz + NZ), NZ)
        owner, side = origin // 2, lax.rem(origin, 2)
        at = slice(i * per, (i + 1) * per)
        out_ref[owner, pl.ds(pl.multiple_of(side * per, per), per), :] += cov_ref[at, :]
        out_ref[owner, own:, :128] += jnp.where(line == side, along_lanes(sq_ref[at, :], 0), 0.0)


def cross(kernel, blocks, ocean, sums_shape, scratch, before=None):
    rows = sum(a.shape[0] for a in blocks)
    depth, cols = blocks[0].shape[1], ocean.shape[1]
    vmem = pl.BlockSpec(memory_space=pltpu.VMEM)
    args = list(blocks) + [ocean]
    specs = [pl.BlockSpec(memory_space=pl.ANY)] * len(blocks) + [vmem]
    if before is not None:
        args.append(before)
        specs.append(vmem)
    return pl.pallas_call(
        kernel,
        out_shape=jax.ShapeDtypeStruct(sums_shape, jnp.float32),
        in_specs=specs,
        out_specs=vmem,
        scratch_shapes=[pltpu.VMEM((rows, depth), jnp.bfloat16)]
        + [pltpu.VMEM((rows, width), jnp.float32) for width in scratch]
        + [pltpu.SemaphoreType.DMA((len(blocks),))],
        input_output_aliases={} if before is None else {len(args) - 1: 0},
        compiler_params=pltpu.CompilerParams(vmem_limit_bytes=24 * 1024 * 1024),
        cost_estimate=pl.CostEstimate(
            flops=2 * rows * depth * cols, bytes_accessed=2 * depth * (rows + cols), transcendentals=0
        ),
    )(*args)


def finish_kernel(members, parts_ref, cutoff_ref, index_ref, table_ref, out_ref):
    own, cols = out_ref.shape
    total = jnp.sum(parts_ref[...], axis=0)
    eye = lax.broadcasted_iota(jnp.int32, (own, own), 0) == lax.broadcasted_iota(jnp.int32, (own, own), 1)
    half = own // 2
    across = jnp.concatenate([total[own : own + 1, :half], total[own + 1 : own + 2, :half]], axis=1)
    rowsq = jnp.sum(jnp.where(eye, across, 0.0), axis=1, keepdims=True)
    vx = rowsq / (members - 1.0) + 1e-06
    vy = total[own + 2 : own + 3] / (members - 1.0) + 1e-06
    corr = total[:own] / (members - 1.0) / jnp.sqrt(vx * vy)
    for i in range(own // TR):
        for j in range(cols // TV):
            weight = cutoff_ref[i, j].astype(jnp.float32) * table_ref[index_ref[i, j]]
            tile = (slice(i * TR, (i + 1) * TR), slice(j * TV, (j + 1) * TV))
            out_ref[tile] = corr[tile] * weight


def per_device(panel, ocean, cutoff, factor_index, factor_table):
    n_mem = lax.axis_size("mem")
    rows_all = panel.shape[1] * lax.axis_size("ocn")
    own_rows = rows_all // n_mem
    members = panel.shape[0] * n_mem
    mine = panel.T
    per = mine.shape[0]
    half = per // 2
    lo, hi = (0, half), (half, half)
    head, tail = mine[:, :-TAIL], mine[:, -TAIL:]
    first = jnp.concatenate([head, y_shift(head, 1)], axis=0)
    second = jnp.concatenate([y_shift(head, -1), y_shift(head, 2)], axis=0)
    tail = z_spread(tail)
    first, second, tail = lax.optimization_barrier((first, second, tail))
    tails = [tail, y_shift(tail, 1), y_shift(tail, -1), y_shift(tail, 2)]

    def parts_1(dz):
        return ((0, dz), (-1, dz))

    def parts_2(dz):
        return ((1, dz), (2, dz))

    early = [(first, parts_1(0)), (second, parts_2(0))]
    late = []
    up_1 = down_1 = first
    up_2 = down_2 = second
    for s in (1, 2, 3):
        up_1, down_1 = z_shift(up_1, 1), z_shift(down_1, -1)
        up_2, down_2 = z_shift(up_2, 1), z_shift(down_2, -1)
        (early if s < 3 else late).extend(
            [(up_1, parts_1(-s)), (down_1, parts_1(s)), (up_2, parts_2(-s)), (down_2, parts_2(s))]
        )
    late += [(z_shift(up_1, 1), parts_1(-4)), (z_shift(down_2, -1), parts_2(4))]

    cols = ocean.shape[1]
    sums_shape = (n_mem, own_rows + EXTRA, cols)
    parts = cross(tail_kernel, tails, ocean, sums_shape, ())
    for pieces in (early, late):
        kernel = functools.partial(head_kernel, [g for _, g in pieces])
        parts = cross(kernel, [a for a, _ in pieces], ocean, sums_shape, (cols, 128), parts)
    parts = lax.all_to_all(parts, "mem", split_axis=0, concat_axis=0, tiled=True)
    return pl.pallas_call(
        lambda *refs: finish_kernel(members, *refs),
        out_shape=jax.ShapeDtypeStruct((own_rows, ocean.shape[1]), jnp.float32),
        in_specs=[pl.BlockSpec(memory_space=pltpu.VMEM)] + [pl.BlockSpec(memory_space=pltpu.SMEM)] * 3,
        out_specs=pl.BlockSpec(memory_space=pltpu.VMEM),
        compiler_params=pltpu.CompilerParams(vmem_limit_bytes=16 * 1024 * 1024),
    )(parts, cutoff, factor_index, factor_table)


def solution(mesh):
    in_specs = (P("mem", "ocn"), P("mem", "ocn"), P("mem", "ocn"), P("mem", "ocn"), P())
    out_specs = P("mem", "ocn")
    return jax.shard_map(
        per_device, mesh=mesh, in_specs=in_specs, out_specs=out_specs, check_vma=False
    )
```

```python
import functools

import jax
import jax.numpy as jnp
from jax import lax
from jax.experimental import pallas as pl
from jax.experimental.pallas import tpu as pltpu
from jax.sharding import PartitionSpec as P

TR = 64
TV = 128
NZ = 8
NY = 4
EXTRA = 8


def z_shift(x, d):
    perm = [(o, (o // NZ) * NZ + (o % NZ + d) % NZ) for o in range(NY * NZ)]
    return lax.ppermute(x, "ocn", perm)


def y_shift(x, d):
    perm = [(o, ((o // NZ + d) % NY) * NZ + o % NZ) for o in range(NY * NZ)]
    return lax.ppermute(x, "ocn", perm)


def square_sums(rows):
    rows_f = rows.astype(jnp.float32)
    return jnp.sum(rows_f * rows_f, axis=1, keepdims=True)


def along_lanes(column):
    shape = (column.shape[0], 128)
    here = lax.broadcasted_iota(jnp.int32, shape, 0) == lax.broadcasted_iota(jnp.int32, shape, 1)
    return jnp.sum(jnp.where(here, column, 0.0), axis=0, keepdims=True)


def cross_kernel(groups, starts, *refs):
    n = len(groups)
    blocks, near_ref, side_ref = refs[:n], refs[n], refs[n + 1]
    out_ref, rows_ref, cov_ref, sq_ref, sem = refs[-5:]
    own = out_ref.shape[2] - EXTRA
    per = own // 2
    cols = near_ref.shape[1]
    copies, placed = [], []
    for ref, parts in zip(blocks, groups):
        to = pl.ds(len(placed) * per, ref.shape[0])
        copies.append(pltpu.make_async_copy(ref, rows_ref.at[to], sem.at[len(copies)]))
        placed.extend(parts)
    for c in copies:
        c.start()
    if starts:
        line = lax.broadcasted_iota(jnp.int32, (EXTRA, cols), 0)
        for i, ref in enumerate((near_ref, side_ref)):
            ocean_f = ref[...].astype(jnp.float32)
            lines = jnp.where(line == 2, jnp.sum(ocean_f * ocean_f, axis=0, keepdims=True), 0.0)
            for m in range(2 * out_ref.shape[1]):
                out_ref[m % 2, m // 2, own:, i * cols : (i + 1) * cols] = lines
    for c in copies:
        c.wait()
    tile = rows_ref.shape[0] // 2

    @pl.loop(0, 2)
    def _(t):
        part = pl.ds(pl.multiple_of(t * tile, 16), tile)
        rows = rows_ref[part, :]
        cov_ref[part, :cols] = jnp.dot(rows, near_ref[...], preferred_element_type=jnp.float32)
        cov_ref[part, cols:] = jnp.dot(rows, side_ref[...], preferred_element_type=jnp.float32)
        sq_ref[part, :] = jnp.broadcast_to(square_sums(rows), (tile, 128))

    o = lax.axis_index("ocn")
    y, z = o // NZ, lax.rem(o, NZ)
    line = lax.broadcasted_iota(jnp.int32, (EXTRA, 128), 0)
    core = lax.rem(lax.axis_index("mem"), 2)
    for i, (dy, dz) in enumerate(placed):
        origin = lax.rem(y + (dy + NY), NY) * NZ + lax.rem(z + (dz + NZ), NZ)
        owner, side = origin // 2, lax.rem(origin, 2)
        to = (lax.rem(owner + core, 2), owner // 2)
        at = slice(i * per, (i + 1) * per)
        out_ref[(*to, pl.ds(pl.multiple_of(side * per, per), per))] = cov_ref[at, :]
        lines = jnp.where(line == side, along_lanes(sq_ref[at, :]), 0.0)
        out_ref[(*to, slice(own, None), slice(0, 128))] += lines
        out_ref[(*to, slice(own, None), slice(cols, cols + 128))] += lines


def cross(pieces, near, side, sums_shape, before=None):
    blocks, groups = [a for a, _ in pieces], [g for _, g in pieces]
    rows = sum(a.shape[0] for a in blocks)
    depth, cols = blocks[0].shape[1], near.shape[1] + side.shape[1]
    vmem = pl.BlockSpec(memory_space=pltpu.VMEM)
    args = blocks + [near, side]
    specs = [pl.BlockSpec(memory_space=pl.ANY)] * len(blocks) + [vmem, vmem]
    if before is not None:
        args.append(before)
        specs.append(vmem)
    return pl.pallas_call(
        functools.partial(cross_kernel, groups, before is None),
        out_shape=jax.ShapeDtypeStruct(sums_shape, jnp.float32),
        in_specs=specs,
        out_specs=vmem,
        scratch_shapes=[
            pltpu.VMEM((rows, depth), jnp.bfloat16),
            pltpu.VMEM((rows, cols), jnp.float32),
            pltpu.VMEM((rows, 128), jnp.float32),
            pltpu.SemaphoreType.DMA((len(blocks),)),
        ],
        input_output_aliases={} if before is None else {len(args) - 1: 0},
        compiler_params=pltpu.CompilerParams(vmem_limit_bytes=24 * 1024 * 1024),
        cost_estimate=pl.CostEstimate(
            flops=2 * rows * depth * cols, bytes_accessed=2 * depth * (rows + cols), transcendentals=0
        ),
    )(*args)


def sum_kernel(parts_ref, near_ref, left_ref, right_ref):
    total = jnp.sum(parts_ref[...], axis=0)
    cols = near_ref.shape[1]
    near_ref[...] = total[:, :cols]
    left_ref[...] = total[:, cols : cols + cols // 2]
    right_ref[...] = total[:, cols + cols // 2 :]


def finish_kernel(members, near_ref, low_ref, high_ref, cutoff_ref, index_ref, table_ref, out_ref):
    own, cols = out_ref.shape
    half = own // 2
    total = near_ref[...] + jnp.concatenate([low_ref[...], high_ref[...]], axis=1)
    squares = near_ref[own:, :128] + high_ref[own:, :]
    eye = lax.broadcasted_iota(jnp.int32, (own, own), 0) == lax.broadcasted_iota(jnp.int32, (own, own), 1)
    across = jnp.concatenate([squares[:1, :half], squares[1:2, :half]], axis=1)
    rowsq = jnp.sum(jnp.where(eye, across, 0.0), axis=1, keepdims=True)
    vx = rowsq / (members - 1.0) + 1e-06
    vy = total[own + 2 : own + 3] / (members - 1.0) + 1e-06
    corr = total[:own] / (members - 1.0) / jnp.sqrt(vx * vy)
    for i in range(own // TR):
        for j in range(cols // TV):
            weight = cutoff_ref[i, j].astype(jnp.float32) * table_ref[index_ref[i, j]]
            tile = (slice(i * TR, (i + 1) * TR), slice(j * TV, (j + 1) * TV))
            out_ref[tile] = corr[tile] * weight


def per_device(panel, ocean, cutoff, factor_index, factor_table):
    n_mem = lax.axis_size("mem")
    own_rows = panel.shape[1] * lax.axis_size("ocn") // n_mem
    members = panel.shape[0] * n_mem
    half, cols = panel.shape[0] // 2, ocean.shape[1]
    parity = lax.rem(lax.axis_index("ocn") // NZ, 2)
    mine = panel.T
    kept = lax.dynamic_slice_in_dim(mine, parity * half, half, 1)
    other = lax.dynamic_slice_in_dim(mine, (1 - parity) * half, half, 1)
    below, above, across = y_shift(other, 1), y_shift(other, -1), y_shift(kept, 2)
    first = jnp.concatenate([kept, below], axis=0)
    second = jnp.concatenate([above, across], axis=0)

    near = lax.dynamic_slice_in_dim(ocean, parity * half, half, 0)
    away = lax.dynamic_slice_in_dim(ocean, (1 - parity) * half, half, 0)
    below, away = lax.optimization_barrier((below, away))
    left, right = y_shift(away[:, cols // 2 :], 1), y_shift(away[:, : cols // 2], -1)
    side = jnp.concatenate([left, right], axis=1)

    def parts_1(dz):
        return ((0, dz), (-1, dz))

    def parts_2(dz):
        return ((1, dz), (2, dz))

    early = [(first, parts_1(0)), (second, parts_2(0))]
    late = []
    up_1 = down_1 = first
    up_2 = down_2 = second
    for s in (1, 2, 3):
        up_1, down_1 = z_shift(up_1, 1), z_shift(down_1, -1)
        up_2, down_2 = z_shift(up_2, 1), z_shift(down_2, -1)
        if s == 2:
            up_1, side = lax.optimization_barrier((up_1, side))
        (early if s < 3 else late).extend(
            [(up_1, parts_1(-s)), (down_1, parts_1(s)), (up_2, parts_2(-s)), (down_2, parts_2(s))]
        )
    late += [(z_shift(up_1, 1), parts_1(-4)), (z_shift(down_2, -1), parts_2(4))]

    sums_shape = (2, n_mem // 2, own_rows + EXTRA, 2 * cols)
    parts = cross(early, near, side, sums_shape)
    parts = cross(late, near, side, sums_shape, parts)
    parts = parts[0] + lax.ppermute(parts[1], "mem", [(m, m ^ 1) for m in range(n_mem)])
    groups = [list(range(c, n_mem, 2)) for c in range(2)]
    parts = lax.all_to_all(parts, "mem", split_axis=0, concat_axis=0, axis_index_groups=groups, tiled=True)
    vmem, smem = pl.BlockSpec(memory_space=pltpu.VMEM), pl.BlockSpec(memory_space=pltpu.SMEM)
    compiler_params = pltpu.CompilerParams(vmem_limit_bytes=16 * 1024 * 1024)
    here, to_left, to_right = pl.pallas_call(
        sum_kernel,
        out_shape=[jax.ShapeDtypeStruct((own_rows + EXTRA, n), jnp.float32) for n in (cols, cols // 2, cols // 2)],
        in_specs=[vmem],
        out_specs=[vmem] * 3,
        compiler_params=compiler_params,
    )(parts)
    low, high = y_shift(to_right, 1), y_shift(to_left, -1)
    return pl.pallas_call(
        functools.partial(finish_kernel, members),
        out_shape=jax.ShapeDtypeStruct((own_rows, cols), jnp.float32),
        in_specs=[vmem] * 3 + [smem] * 3,
        out_specs=vmem,
        compiler_params=compiler_params,
    )(here, low, high, cutoff, factor_index, factor_table)


def solution(mesh):
    in_specs = (P("mem", "ocn"), P("mem", "ocn"), P("mem", "ocn"), P("mem", "ocn"), P())
    out_specs = P("mem", "ocn")
    return jax.shard_map(
        per_device, mesh=mesh, in_specs=in_specs, out_specs=out_specs, check_vma=False
    )
```

```python
import functools

import jax
import jax.numpy as jnp
from jax import lax
from jax.experimental import pallas as pl
from jax.experimental.pallas import tpu as pltpu
from jax.sharding import PartitionSpec as P

TR = 64
TV = 128
NZ = 8
NY = 4
EXTRA = 8


def z_shift(x, d):
    perm = [(o, (o // NZ) * NZ + (o % NZ + d) % NZ) for o in range(NY * NZ)]
    return lax.ppermute(x, "ocn", perm)


def y_shift(x, d):
    perm = [(o, ((o // NZ + d) % NY) * NZ + o % NZ) for o in range(NY * NZ)]
    return lax.ppermute(x, "ocn", perm)


def square_sums(rows):
    rows_f = rows.astype(jnp.float32)
    return jnp.sum(rows_f * rows_f, axis=1, keepdims=True)


def along_lanes(column):
    shape = (column.shape[0], 128)
    here = lax.broadcasted_iota(jnp.int32, shape, 0) == lax.broadcasted_iota(jnp.int32, shape, 1)
    return jnp.sum(jnp.where(here, column, 0.0), axis=0, keepdims=True)


def cross_kernel(groups, starts, *refs):
    n = len(groups)
    blocks, near_ref, side_ref = refs[:n], refs[n], refs[n + 1]
    out_ref, rows_ref, cov_ref, sq_ref, sem = refs[-5:]
    own = out_ref.shape[2] - EXTRA
    per = own // 2
    cols = near_ref.shape[1]
    copies, placed = [], []
    for ref, parts in zip(blocks, groups):
        to = pl.ds(len(placed) * per, ref.shape[0])
        copies.append(pltpu.make_async_copy(ref, rows_ref.at[to], sem.at[len(copies)]))
        placed.extend(parts)
    for c in copies:
        c.start()
    if starts:
        line = lax.broadcasted_iota(jnp.int32, (EXTRA, cols), 0)
        for i, ref in enumerate((near_ref, side_ref)):
            ocean_f = ref[...].astype(jnp.float32)
            lines = jnp.where(line == 2, jnp.sum(ocean_f * ocean_f, axis=0, keepdims=True), 0.0)
            for m in range(2 * out_ref.shape[1]):
                out_ref[m % 2, m // 2, own:, i * cols : (i + 1) * cols] = lines
    for c in copies:
        c.wait()
    tile = rows_ref.shape[0] // 2

    @pl.loop(0, 2)
    def _(t):
        part = pl.ds(pl.multiple_of(t * tile, 16), tile)
        rows = rows_ref[part, :]
        cov_ref[part, :cols] = jnp.dot(rows, near_ref[...], preferred_element_type=jnp.float32)
        cov_ref[part, cols:] = jnp.dot(rows, side_ref[...], preferred_element_type=jnp.float32)
        sq_ref[part, :] = jnp.broadcast_to(square_sums(rows), (tile, 128))

    o = lax.axis_index("ocn")
    y, z = o // NZ, lax.rem(o, NZ)
    line = lax.broadcasted_iota(jnp.int32, (EXTRA, 128), 0)
    core = lax.rem(lax.axis_index("mem"), 2)
    for i, (dy, dz) in enumerate(placed):
        origin = lax.rem(y + (dy + NY), NY) * NZ + lax.rem(z + (dz + NZ), NZ)
        owner, side = origin // 2, lax.rem(origin, 2)
        to = (lax.rem(owner + core, 2), owner // 2)
        at = slice(i * per, (i + 1) * per)
        out_ref[(*to, pl.ds(pl.multiple_of(side * per, per), per))] = cov_ref[at, :]
        lines = jnp.where(line == side, along_lanes(sq_ref[at, :]), 0.0)
        out_ref[(*to, slice(own, None), slice(0, 128))] += lines
        out_ref[(*to, slice(own, None), slice(cols, cols + 128))] += lines


def cross(pieces, near, side, sums_shape, before=None):
    blocks, groups = [a for a, _ in pieces], [g for _, g in pieces]
    rows = sum(a.shape[0] for a in blocks)
    depth, cols = blocks[0].shape[1], near.shape[1] + side.shape[1]
    vmem = pl.BlockSpec(memory_space=pltpu.VMEM)
    args = blocks + [near, side]
    specs = [pl.BlockSpec(memory_space=pl.ANY)] * len(blocks) + [vmem, vmem]
    if before is not None:
        args.append(before)
        specs.append(vmem)
    return pl.pallas_call(
        functools.partial(cross_kernel, groups, before is None),
        out_shape=jax.ShapeDtypeStruct(sums_shape, jnp.float32),
        in_specs=specs,
        out_specs=vmem,
        scratch_shapes=[
            pltpu.VMEM((rows, depth), jnp.bfloat16),
            pltpu.VMEM((rows, cols), jnp.float32),
            pltpu.VMEM((rows, 128), jnp.float32),
            pltpu.SemaphoreType.DMA((len(blocks),)),
        ],
        input_output_aliases={} if before is None else {len(args) - 1: 0},
        compiler_params=pltpu.CompilerParams(vmem_limit_bytes=24 * 1024 * 1024),
        cost_estimate=pl.CostEstimate(
            flops=2 * rows * depth * cols, bytes_accessed=2 * depth * (rows + cols), transcendentals=0
        ),
    )(*args)


def sum_kernel(parts_ref, near_ref, left_ref, right_ref):
    total = jnp.sum(parts_ref[...], axis=0)
    cols = near_ref.shape[1]
    near_ref[...] = total[:, :cols]
    left_ref[...] = total[:, cols : cols + cols // 2]
    right_ref[...] = total[:, cols + cols // 2 :]


def finish_kernel(members, near_ref, low_ref, high_ref, cutoff_ref, index_ref, table_ref, out_ref):
    own, cols = out_ref.shape
    half = own // 2
    total = near_ref[...] + jnp.concatenate([low_ref[...], high_ref[...]], axis=1)
    squares = near_ref[own:, :128] + high_ref[own:, :]
    eye = lax.broadcasted_iota(jnp.int32, (own, own), 0) == lax.broadcasted_iota(jnp.int32, (own, own), 1)
    across = jnp.concatenate([squares[:1, :half], squares[1:2, :half]], axis=1)
    rowsq = jnp.sum(jnp.where(eye, across, 0.0), axis=1, keepdims=True)
    vx = rowsq / (members - 1.0) + 1e-06
    vy = total[own + 2 : own + 3] / (members - 1.0) + 1e-06
    corr = total[:own] / (members - 1.0) / jnp.sqrt(vx * vy)
    for i in range(own // TR):
        for j in range(cols // TV):
            weight = cutoff_ref[i, j].astype(jnp.float32) * table_ref[index_ref[i, j]]
            tile = (slice(i * TR, (i + 1) * TR), slice(j * TV, (j + 1) * TV))
            out_ref[tile] = corr[tile] * weight


def per_device(panel, ocean, cutoff, factor_index, factor_table):
    n_mem = lax.axis_size("mem")
    own_rows = panel.shape[1] * lax.axis_size("ocn") // n_mem
    members = panel.shape[0] * n_mem
    half, cols = panel.shape[0] // 2, ocean.shape[1]
    parity = lax.rem(lax.axis_index("ocn") // NZ, 2)
    mine = panel.T
    kept = lax.dynamic_slice_in_dim(mine, parity * half, half, 1)
    other = lax.dynamic_slice_in_dim(mine, (1 - parity) * half, half, 1)
    below, above, across = y_shift(other, 1), y_shift(other, -1), y_shift(kept, 2)
    first = jnp.concatenate([kept, below], axis=0)
    second = jnp.concatenate([above, across], axis=0)

    near = lax.dynamic_slice_in_dim(ocean, parity * half, half, 0)
    away = lax.dynamic_slice_in_dim(ocean, (1 - parity) * half, half, 0)
    below, away = lax.optimization_barrier((below, away))
    left, right = y_shift(away[:, cols // 2 :], 1), y_shift(away[:, : cols // 2], -1)
    side = jnp.concatenate([left, right], axis=1)

    def parts_1(dz):
        return ((0, dz), (-1, dz))

    def parts_2(dz):
        return ((1, dz), (2, dz))

    early = [(first, parts_1(0)), (second, parts_2(0))]
    late = []
    up_1 = down_1 = first
    up_2 = down_2 = second
    for s in (1, 2, 3):
        up_1, down_1 = z_shift(up_1, 1), z_shift(down_1, -1)
        up_2, down_2 = z_shift(up_2, 1), z_shift(down_2, -1)
        if s == 1:
            down_1, side = lax.optimization_barrier((down_1, side))
        (early if s < 3 else late).extend(
            [(up_1, parts_1(-s)), (down_1, parts_1(s)), (up_2, parts_2(-s)), (down_2, parts_2(s))]
        )
    late += [(z_shift(up_1, 1), parts_1(-4)), (z_shift(down_2, -1), parts_2(4))]

    sums_shape = (2, n_mem // 2, own_rows + EXTRA, 2 * cols)
    parts = cross(early, near, side, sums_shape)
    parts = cross(late, near, side, sums_shape, parts)
    parts = parts[0] + lax.ppermute(parts[1], "mem", [(m, m ^ 1) for m in range(n_mem)])
    groups = [list(range(c, n_mem, 2)) for c in range(2)]
    parts = lax.all_to_all(parts, "mem", split_axis=0, concat_axis=0, axis_index_groups=groups, tiled=True)
    vmem, smem = pl.BlockSpec(memory_space=pltpu.VMEM), pl.BlockSpec(memory_space=pltpu.SMEM)
    compiler_params = pltpu.CompilerParams(vmem_limit_bytes=16 * 1024 * 1024)
    here, to_left, to_right = pl.pallas_call(
        sum_kernel,
        out_shape=[jax.ShapeDtypeStruct((own_rows + EXTRA, n), jnp.float32) for n in (cols, cols // 2, cols // 2)],
        in_specs=[vmem],
        out_specs=[vmem] * 3,
        compiler_params=compiler_params,
    )(parts)
    low, high = y_shift(to_right, 1), y_shift(to_left, -1)
    return pl.pallas_call(
        functools.partial(finish_kernel, members),
        out_shape=jax.ShapeDtypeStruct((own_rows, cols), jnp.float32),
        in_specs=[vmem] * 3 + [smem] * 3,
        out_specs=vmem,
        compiler_params=compiler_params,
    )(here, low, high, cutoff, factor_index, factor_table)


def solution(mesh):
    in_specs = (P("mem", "ocn"), P("mem", "ocn"), P("mem", "ocn"), P("mem", "ocn"), P())
    out_specs = P("mem", "ocn")
    return jax.shard_map(
        per_device, mesh=mesh, in_specs=in_specs, out_specs=out_specs, check_vma=False
    )
```

```python
import functools

import jax
import jax.numpy as jnp
from jax import lax
from jax.experimental import pallas as pl
from jax.experimental.pallas import tpu as pltpu
from jax.sharding import PartitionSpec as P

TR = 64
TV = 128
NZ = 8
NY = 4
EXTRA = 8


def z_shift(x, d):
    perm = [(o, (o // NZ) * NZ + (o % NZ + d) % NZ) for o in range(NY * NZ)]
    return lax.ppermute(x, "ocn", perm)


def y_shift(x, d):
    perm = [(o, ((o // NZ + d) % NY) * NZ + o % NZ) for o in range(NY * NZ)]
    return lax.ppermute(x, "ocn", perm)


def square_sums(rows):
    rows_f = rows.astype(jnp.float32)
    return jnp.sum(rows_f * rows_f, axis=1, keepdims=True)


def along_lanes(column):
    shape = (column.shape[0], 128)
    here = lax.broadcasted_iota(jnp.int32, shape, 0) == lax.broadcasted_iota(jnp.int32, shape, 1)
    return jnp.sum(jnp.where(here, column, 0.0), axis=0, keepdims=True)


def cross_kernel(groups, starts, *refs):
    n = len(groups)
    blocks, near_ref, side_ref = refs[:n], refs[n], refs[n + 1]
    out_ref, rows_ref, cov_ref, sq_ref, sem = refs[-5:]
    own = out_ref.shape[3] - EXTRA
    per = own // 2
    cols = near_ref.shape[1]
    copies, placed = [], []
    for ref, parts in zip(blocks, groups):
        to = pl.ds(len(placed) * per, ref.shape[0])
        copies.append(pltpu.make_async_copy(ref, rows_ref.at[to], sem.at[len(copies)]))
        placed.extend(parts)
    for c in copies:
        c.start()
    if starts:
        line = lax.broadcasted_iota(jnp.int32, (EXTRA, cols), 0)
        for i, ref in enumerate((near_ref, side_ref)):
            ocean_f = ref[...].astype(jnp.float32)
            lines = jnp.where(line == 2, jnp.sum(ocean_f * ocean_f, axis=0, keepdims=True), 0.0)
            for m in range(2 * out_ref.shape[2]):
                out_ref[m % 2, i, m // 2, own:, :] = lines
    for c in copies:
        c.wait()
    tile = rows_ref.shape[0] // 2

    @pl.loop(0, 2)
    def _(t):
        part = pl.ds(pl.multiple_of(t * tile, 16), tile)
        rows = rows_ref[part, :]
        cov_ref[part, :cols] = jnp.dot(rows, near_ref[...], preferred_element_type=jnp.float32)
        cov_ref[part, cols:] = jnp.dot(rows, side_ref[...], preferred_element_type=jnp.float32)
        sq_ref[part, :] = jnp.broadcast_to(square_sums(rows), (tile, 128))

    o = lax.axis_index("ocn")
    y, z = o // NZ, lax.rem(o, NZ)
    line = lax.broadcasted_iota(jnp.int32, (EXTRA, 128), 0)
    core = lax.rem(lax.axis_index("mem"), 2)
    for i, (dy, dz) in enumerate(placed):
        origin = lax.rem(y + (dy + NY), NY) * NZ + lax.rem(z + (dz + NZ), NZ)
        owner, side = origin // 2, lax.rem(origin, 2)
        whose, chip = lax.rem(owner + core, 2), owner // 2
        at = slice(i * per, (i + 1) * per)
        to = pl.ds(pl.multiple_of(side * per, per), per)
        lines = jnp.where(line == side, along_lanes(sq_ref[at, :]), 0.0)
        for j in range(2):
            out_ref[whose, j, chip, to, :] = cov_ref[at, j * cols : (j + 1) * cols]
            out_ref[whose, j, chip, own:, :128] += lines


def cross(pieces, near, side, sums_shape, before=None):
    blocks, groups = [a for a, _ in pieces], [g for _, g in pieces]
    rows = sum(a.shape[0] for a in blocks)
    depth, cols = blocks[0].shape[1], near.shape[1] + side.shape[1]
    vmem = pl.BlockSpec(memory_space=pltpu.VMEM)
    args = blocks + [near, side]
    specs = [pl.BlockSpec(memory_space=pl.ANY)] * len(blocks) + [vmem, vmem]
    if before is not None:
        args.append(before)
        specs.append(vmem)
    return pl.pallas_call(
        functools.partial(cross_kernel, groups, before is None),
        out_shape=jax.ShapeDtypeStruct(sums_shape, jnp.float32),
        in_specs=specs,
        out_specs=vmem,
        scratch_shapes=[
            pltpu.VMEM((rows, depth), jnp.bfloat16),
            pltpu.VMEM((rows, cols), jnp.float32),
            pltpu.VMEM((rows, 128), jnp.float32),
            pltpu.SemaphoreType.DMA((len(blocks),)),
        ],
        input_output_aliases={} if before is None else {len(args) - 1: 0},
        compiler_params=pltpu.CompilerParams(vmem_limit_bytes=24 * 1024 * 1024),
        cost_estimate=pl.CostEstimate(
            flops=2 * rows * depth * cols, bytes_accessed=2 * depth * (rows + cols), transcendentals=0
        ),
    )(*args)


def sides_kernel(parts_ref, left_ref, right_ref):
    total = jnp.sum(parts_ref[...], axis=0)
    cols = total.shape[1] // 2
    left_ref[...] = total[:, :cols]
    right_ref[...] = total[:, cols:]


def finish_kernel(members, parts_ref, low_ref, high_ref, cutoff_ref, index_ref, table_ref, out_ref):
    own, cols = out_ref.shape
    half = own // 2
    near = jnp.sum(parts_ref[...], axis=0)
    total = near + jnp.concatenate([low_ref[...], high_ref[...]], axis=1)
    squares = near[own:, :128] + high_ref[own:, :]
    eye = lax.broadcasted_iota(jnp.int32, (own, own), 0) == lax.broadcasted_iota(jnp.int32, (own, own), 1)
    across = jnp.concatenate([squares[:1, :half], squares[1:2, :half]], axis=1)
    rowsq = jnp.sum(jnp.where(eye, across, 0.0), axis=1, keepdims=True)
    vx = rowsq / (members - 1.0) + 1e-06
    vy = total[own + 2 : own + 3] / (members - 1.0) + 1e-06
    corr = total[:own] / (members - 1.0) / jnp.sqrt(vx * vy)
    for i in range(own // TR):
        for j in range(cols // TV):
            weight = cutoff_ref[i, j].astype(jnp.float32) * table_ref[index_ref[i, j]]
            tile = (slice(i * TR, (i + 1) * TR), slice(j * TV, (j + 1) * TV))
            out_ref[tile] = corr[tile] * weight


def per_device(panel, ocean, cutoff, factor_index, factor_table):
    n_mem = lax.axis_size("mem")
    own_rows = panel.shape[1] * lax.axis_size("ocn") // n_mem
    members = panel.shape[0] * n_mem
    half, cols = panel.shape[0] // 2, ocean.shape[1]
    parity = lax.rem(lax.axis_index("ocn") // NZ, 2)
    mine = panel.T
    kept = lax.dynamic_slice_in_dim(mine, parity * half, half, 1)
    other = lax.dynamic_slice_in_dim(mine, (1 - parity) * half, half, 1)
    below, above, across = y_shift(other, 1), y_shift(other, -1), y_shift(kept, 2)
    first = jnp.concatenate([kept, below], axis=0)
    second = jnp.concatenate([above, across], axis=0)

    near = lax.dynamic_slice_in_dim(ocean, parity * half, half, 0)
    away = lax.dynamic_slice_in_dim(ocean, (1 - parity) * half, half, 0)
    below, away = lax.optimization_barrier((below, away))
    left, right = y_shift(away[:, cols // 2 :], 1), y_shift(away[:, : cols // 2], -1)
    side = jnp.concatenate([left, right], axis=1)

    def parts_1(dz):
        return ((0, dz), (-1, dz))

    def parts_2(dz):
        return ((1, dz), (2, dz))

    early = [(first, parts_1(0)), (second, parts_2(0))]
    late = []
    up_1 = down_1 = first
    up_2 = down_2 = second
    for s in (1, 2, 3):
        up_1, down_1 = z_shift(up_1, 1), z_shift(down_1, -1)
        up_2, down_2 = z_shift(up_2, 1), z_shift(down_2, -1)
        if s == 1:
            down_1, side = lax.optimization_barrier((down_1, side))
        (early if s < 3 else late).extend(
            [(up_1, parts_1(-s)), (down_1, parts_1(s)), (up_2, parts_2(-s)), (down_2, parts_2(s))]
        )
    late += [(z_shift(up_1, 1), parts_1(-4)), (z_shift(down_2, -1), parts_2(4))]

    sums_shape = (2, 2, n_mem // 2, own_rows + EXTRA, cols)
    parts = cross(early, near, side, sums_shape)
    parts = cross(late, near, side, sums_shape, parts)
    received = lax.ppermute(parts[1], "mem", [(m, m ^ 1) for m in range(n_mem)])
    groups = [list(range(c, n_mem, 2)) for c in range(2)]
    exchange = functools.partial(
        lax.all_to_all, axis_name="mem", split_axis=0, concat_axis=0, axis_index_groups=groups, tiled=True
    )
    side_parts = exchange(parts[0, 1] + received[1])
    near_parts = exchange(parts[0, 0] + received[0])
    vmem, smem = pl.BlockSpec(memory_space=pltpu.VMEM), pl.BlockSpec(memory_space=pltpu.SMEM)
    compiler_params = pltpu.CompilerParams(vmem_limit_bytes=16 * 1024 * 1024)
    to_left, to_right = pl.pallas_call(
        sides_kernel,
        out_shape=[jax.ShapeDtypeStruct((own_rows + EXTRA, cols // 2), jnp.float32)] * 2,
        in_specs=[vmem],
        out_specs=[vmem] * 2,
        compiler_params=compiler_params,
    )(side_parts)
    low, high = y_shift(to_right, 1), y_shift(to_left, -1)
    return pl.pallas_call(
        functools.partial(finish_kernel, members),
        out_shape=jax.ShapeDtypeStruct((own_rows, cols), jnp.float32),
        in_specs=[vmem] * 3 + [smem] * 3,
        out_specs=vmem,
        compiler_params=compiler_params,
    )(near_parts, low, high, cutoff, factor_index, factor_table)


def solution(mesh):
    in_specs = (P("mem", "ocn"), P("mem", "ocn"), P("mem", "ocn"), P("mem", "ocn"), P())
    out_specs = P("mem", "ocn")
    return jax.shard_map(
        per_device, mesh=mesh, in_specs=in_specs, out_specs=out_specs, check_vma=False
    )
```

```python
import functools

import jax
import jax.numpy as jnp
from jax import lax
from jax.experimental import pallas as pl
from jax.experimental.pallas import tpu as pltpu
from jax.sharding import PartitionSpec as P

TR = 64
TV = 128
NZ = 8
NY = 4
EXTRA = 8


def z_shift(x, d):
    perm = [(o, (o // NZ) * NZ + (o % NZ + d) % NZ) for o in range(NY * NZ)]
    return lax.ppermute(x, "ocn", perm)


def y_shift(x, d):
    perm = [(o, ((o // NZ + d) % NY) * NZ + o % NZ) for o in range(NY * NZ)]
    return lax.ppermute(x, "ocn", perm)


def square_sums(rows):
    rows_f = rows.astype(jnp.float32)
    return jnp.sum(rows_f * rows_f, axis=1, keepdims=True)


def along_lanes(column):
    shape = (column.shape[0], 128)
    here = lax.broadcasted_iota(jnp.int32, shape, 0) == lax.broadcasted_iota(jnp.int32, shape, 1)
    return jnp.sum(jnp.where(here, column, 0.0), axis=0, keepdims=True)


def cross_kernel(groups, starts, *refs):
    n = len(groups)
    blocks, near_ref, side_ref = refs[:n], refs[n], refs[n + 1]
    out_ref, rows_ref, cov_ref, sq_ref, sem = refs[-5:]
    own = out_ref.shape[3] - EXTRA
    per = own // 2
    cols = near_ref.shape[1]
    copies, placed = [], []
    for ref, parts in zip(blocks, groups):
        to = pl.ds(len(placed) * per, ref.shape[0])
        copies.append(pltpu.make_async_copy(ref, rows_ref.at[to], sem.at[len(copies)]))
        placed.extend(parts)
    for c in copies:
        c.start()
    if starts:
        line = lax.broadcasted_iota(jnp.int32, (EXTRA, cols), 0)
        for i, ref in enumerate((near_ref, side_ref)):
            ocean_f = ref[...].astype(jnp.float32)
            lines = jnp.where(line == 2, jnp.sum(ocean_f * ocean_f, axis=0, keepdims=True), 0.0)
            for m in range(2 * out_ref.shape[2]):
                out_ref[m % 2, i, m // 2, own:, :] = lines
    for c in copies:
        c.wait()
    tile = rows_ref.shape[0] // 2

    @pl.loop(0, 2)
    def _(t):
        part = pl.ds(pl.multiple_of(t * tile, 16), tile)
        rows = rows_ref[part, :]
        cov_ref[part, :cols] = jnp.dot(rows, near_ref[...], preferred_element_type=jnp.float32)
        cov_ref[part, cols:] = jnp.dot(rows, side_ref[...], preferred_element_type=jnp.float32)
        sq_ref[part, :] = jnp.broadcast_to(square_sums(rows), (tile, 128))

    o = lax.axis_index("ocn")
    y, z = o // NZ, lax.rem(o, NZ)
    line = lax.broadcasted_iota(jnp.int32, (EXTRA, 128), 0)
    core = lax.rem(lax.axis_index("mem"), 2)
    for i, (dy, dz) in enumerate(placed):
        origin = lax.rem(y + (dy + NY), NY) * NZ + lax.rem(z + (dz + NZ), NZ)
        owner, side = origin // 2, lax.rem(origin, 2)
        whose, chip = lax.rem(owner + core, 2), owner // 2
        at = slice(i * per, (i + 1) * per)
        to = pl.ds(pl.multiple_of(side * per, per), per)
        lines = jnp.where(line == side, along_lanes(sq_ref[at, :]), 0.0)
        for j in range(2):
            out_ref[whose, j, chip, to, :] = cov_ref[at, j * cols : (j + 1) * cols]
            out_ref[whose, j, chip, own:, :128] += lines


def cross(pieces, near, side, sums_shape, before=None):
    blocks, groups = [a for a, _ in pieces], [g for _, g in pieces]
    rows = sum(a.shape[0] for a in blocks)
    depth, cols = blocks[0].shape[1], near.shape[1] + side.shape[1]
    vmem = pl.BlockSpec(memory_space=pltpu.VMEM)
    args = blocks + [near, side]
    specs = [pl.BlockSpec(memory_space=pl.ANY)] * len(blocks) + [vmem, vmem]
    if before is not None:
        args.append(before)
        specs.append(vmem)
    return pl.pallas_call(
        functools.partial(cross_kernel, groups, before is None),
        out_shape=jax.ShapeDtypeStruct(sums_shape, jnp.float32),
        in_specs=specs,
        out_specs=vmem,
        scratch_shapes=[
            pltpu.VMEM((rows, depth), jnp.bfloat16),
            pltpu.VMEM((rows, cols), jnp.float32),
            pltpu.VMEM((rows, 128), jnp.float32),
            pltpu.SemaphoreType.DMA((len(blocks),)),
        ],
        input_output_aliases={} if before is None else {len(args) - 1: 0},
        compiler_params=pltpu.CompilerParams(vmem_limit_bytes=24 * 1024 * 1024),
        cost_estimate=pl.CostEstimate(
            flops=2 * rows * depth * cols, bytes_accessed=2 * depth * (rows + cols), transcendentals=0
        ),
    )(*args)


def sides_kernel(parts_ref, left_ref, right_ref):
    total = jnp.sum(parts_ref[...], axis=0)
    cols = total.shape[1] // 2
    left_ref[...] = total[:, :cols]
    right_ref[...] = total[:, cols:]


def finish_kernel(members, parts_ref, low_ref, high_ref, cutoff_ref, index_ref, table_ref, out_ref):
    own, cols = out_ref.shape
    half = own // 2
    near = jnp.sum(parts_ref[...], axis=0)
    total = near + jnp.concatenate([low_ref[...], high_ref[...]], axis=1)
    squares = near[own:, :128] + high_ref[own:, :]
    eye = lax.broadcasted_iota(jnp.int32, (own, own), 0) == lax.broadcasted_iota(jnp.int32, (own, own), 1)
    across = jnp.concatenate([squares[:1, :half], squares[1:2, :half]], axis=1)
    rowsq = jnp.sum(jnp.where(eye, across, 0.0), axis=1, keepdims=True)
    vx = rowsq / (members - 1.0) + 1e-06
    vy = total[own + 2 : own + 3] / (members - 1.0) + 1e-06
    corr = total[:own] / (members - 1.0) / jnp.sqrt(vx * vy)
    for i in range(own // TR):
        for j in range(cols // TV):
            weight = cutoff_ref[i, j].astype(jnp.float32) * table_ref[index_ref[i, j]]
            tile = (slice(i * TR, (i + 1) * TR), slice(j * TV, (j + 1) * TV))
            out_ref[tile] = corr[tile] * weight


def per_device(panel, ocean, cutoff, factor_index, factor_table):
    n_mem = lax.axis_size("mem")
    own_rows = panel.shape[1] * lax.axis_size("ocn") // n_mem
    members = panel.shape[0] * n_mem
    half, cols = panel.shape[0] // 2, ocean.shape[1]
    parity = lax.rem(lax.axis_index("ocn") // NZ, 2)
    mine = panel.T
    kept = lax.dynamic_slice_in_dim(mine, parity * half, half, 1)
    other = lax.dynamic_slice_in_dim(mine, (1 - parity) * half, half, 1)
    below, above, across = y_shift(other, 1), y_shift(other, -1), y_shift(kept, 2)
    first = jnp.concatenate([kept, below], axis=0)
    second = jnp.concatenate([above, across], axis=0)

    near = lax.dynamic_slice_in_dim(ocean, parity * half, half, 0)
    away = lax.dynamic_slice_in_dim(ocean, (1 - parity) * half, half, 0)
    below, away = lax.optimization_barrier((below, away))
    left, right = y_shift(away[:, cols // 2 :], 1), y_shift(away[:, : cols // 2], -1)
    side = jnp.concatenate([left, right], axis=1)

    def parts_1(dz):
        return ((0, dz), (-1, dz))

    def parts_2(dz):
        return ((1, dz), (2, dz))

    early = [(first, parts_1(0)), (second, parts_2(0))]
    late = []
    up_1 = down_1 = first
    up_2 = down_2 = second
    for s in (1, 2, 3):
        up_1, down_1 = z_shift(up_1, 1), z_shift(down_1, -1)
        up_2, down_2 = z_shift(up_2, 1), z_shift(down_2, -1)
        if s == 1:
            down_1, side = lax.optimization_barrier((down_1, side))
        (early if s < 3 else late).extend(
            [(up_1, parts_1(-s)), (down_1, parts_1(s)), (up_2, parts_2(-s)), (down_2, parts_2(s))]
        )
    late += [(z_shift(up_1, 1), parts_1(-4)), (z_shift(down_2, -1), parts_2(4))]

    sums_shape = (2, 2, n_mem // 2, own_rows + EXTRA, cols)
    parts = cross(early, near, side, sums_shape)
    parts = cross(late, near, side, sums_shape, parts)
    def from_other_core(x):
        return lax.ppermute(x, "mem", [(m, m ^ 1) for m in range(n_mem)])

    side_received = from_other_core(parts[1, 1])
    near_received = from_other_core(parts[1, 0])
    groups = [list(range(c, n_mem, 2)) for c in range(2)]
    exchange = functools.partial(
        lax.all_to_all, axis_name="mem", split_axis=0, concat_axis=0, axis_index_groups=groups, tiled=True
    )
    side_parts = exchange(parts[0, 1] + side_received)
    near_parts = exchange(parts[0, 0] + near_received)
    vmem, smem = pl.BlockSpec(memory_space=pltpu.VMEM), pl.BlockSpec(memory_space=pltpu.SMEM)
    compiler_params = pltpu.CompilerParams(vmem_limit_bytes=16 * 1024 * 1024)
    to_left, to_right = pl.pallas_call(
        sides_kernel,
        out_shape=[jax.ShapeDtypeStruct((own_rows + EXTRA, cols // 2), jnp.float32)] * 2,
        in_specs=[vmem],
        out_specs=[vmem] * 2,
        compiler_params=compiler_params,
    )(side_parts)
    low, high = y_shift(to_right, 1), y_shift(to_left, -1)
    return pl.pallas_call(
        functools.partial(finish_kernel, members),
        out_shape=jax.ShapeDtypeStruct((own_rows, cols), jnp.float32),
        in_specs=[vmem] * 3 + [smem] * 3,
        out_specs=vmem,
        compiler_params=compiler_params,
    )(near_parts, low, high, cutoff, factor_index, factor_table)


def solution(mesh):
    in_specs = (P("mem", "ocn"), P("mem", "ocn"), P("mem", "ocn"), P("mem", "ocn"), P())
    out_specs = P("mem", "ocn")
    return jax.shard_map(
        per_device, mesh=mesh, in_specs=in_specs, out_specs=out_specs, check_vma=False
    )
```
